128 devices in a mesh: dp: 32 (over x, z_lo, y), tensor: 4 (over z_hi, core).
Axes of the slice: x: 4, y: 4, z: 4 (z_hi: 2, z_lo: 2; z = z_hi * 2 + z_lo), core: 2. Of those that a mesh axis runs over, the one named last changes fastest.
Arguments:
- teacher_states: bfloat16 [4, 2048, 16384], P(None, 'tensor', 'dp'), as said below
- layer_map: int32 [1], replicated, may hold values from 0 to 3
- token_order: int32 [2048], replicated, may hold values from 0 to 2047, each once
- student_states: bfloat16 [2048, 4096], P('dp', 'tensor'), may hold values from -6 to 6
- teacher_gain: bfloat16 [16384], P('dp'), may hold values from 0.099609375 to 1.8984375
- student_gain: bfloat16 [4096], P('tensor'), may hold values from 0.099609375 to 1.8984375
- adapter: bfloat16 [16384, 4096], P('dp', 'tensor'), may hold values from -0.046875 to 0.046875
- w_gate: bfloat16 [4096, 14336], P('tensor', 'dp'), may hold values from -0.09375 to 0.09375
- w_up: bfloat16 [4096, 14336], P('tensor', 'dp'), may hold values from -0.09375 to 0.09375
- w_down: bfloat16 [14336, 4096], P('dp', 'tensor'), may hold values from -0.046875 to 0.046875
Outputs:
- grad_gate: float32 [4096, 14336], P('tensor', 'dp')
- grad_up: float32 [4096, 14336], P('tensor', 'dp')
- grad_down: float32 [14336, 4096], P('dp', 'tensor')
- grad_adapter: float32 [16384, 4096], P('dp', 'tensor')
The draws below stay inside these ranges and needn't reach their ends.
Inputs may be any that keep to these rules, and one draw needn't show every extreme that they name: `layer_map`: a number of a teacher layer. `token_order`: each teacher token exactly once. `teacher_states`: finite teacher states.
All inputs are finite; a program needn't handle non-finite values.
Results may differ from the reference program's by a relative error of at most 0.0066.
Values may be sent and summed in bfloat16 or wider, within the bound.
No kernel may reach another device: no remote copies, remote signals or barrier semaphores. Data moves between devices by JAX's collectives and lax.ppermute only.
A program may use at most 128 MiB of HBM per device.

```python
import math
import jax
import jax.numpy as jnp
from jax import lax

DT = 16384
D = 4096
FF = 14336
LT = 4
TOKENS = 2048


def draw_teacher_states(key, part):
    key = jax.random.fold_in(key, 11)
    first, second = jax.random.split(key, 2)
    shape = (LT, TOKENS, DT)
    column = 1.0 + 2.0 * jnp.arange(DT, dtype=jnp.float32) / (DT - 1)
    scales = jnp.exp(jax.random.uniform(second, (LT, TOKENS, 1), jnp.float32, 0.0, math.log(10.0)))
    base = jnp.clip(jax.random.normal(first, shape, jnp.float32), -6.0, 6.0)
    return (base * scales * column).astype(jnp.bfloat16)


def block_scale(own_key, dims, cuts, least, high):
    def one(dim, shards_of):
        heights = jax.random.uniform(jax.random.fold_in(jax.random.fold_in(own_key, 6), dim), (shards_of,), jnp.float32, least / len(cuts), high / len(cuts))
        return jnp.repeat(jnp.exp(heights), dims[dim] // shards_of).reshape((-1,) + (1,) * (len(dims) - dim - 1))

    level = one(*cuts[0])
    for cut in cuts[1:]:
        level = level * one(*cut)
    return level


def centred(key, extent, width, reach, cuts=(), kind=jnp.bfloat16):
    entries = width * jax.random.normal(key, extent, jnp.float32)
    if cuts:
        entries = entries * block_scale(key, extent, cuts, -0.22, 0.18)
    return jnp.clip(entries, -reach, reach).astype(kind)


def setup_inputs(seed: int = 0) -> dict:
    key_of = jax.random.split(jax.random.key(seed), 11)
    teacher_states = draw_teacher_states(jax.random.fold_in(key_of[10], 71), 0)
    layer_map = jax.random.randint(key_of[1], (1,), 0, LT).astype(jnp.int32)
    token_order = jax.random.permutation(key_of[2], TOKENS).astype(jnp.int32)
    student_states = centred(key_of[3], (TOKENS, D), 1.0, 6.0, ((0, 32), (1, 4)))
    teacher_gain = jnp.clip(1.0 + 0.18 * jax.random.normal(key_of[4], (DT,), jnp.float32), 0.099609375, 1.8984375).astype(jnp.bfloat16)
    student_gain = jnp.clip(1.0 + 0.18 * jax.random.normal(key_of[5], (D,), jnp.float32), 0.099609375, 1.8984375).astype(jnp.bfloat16)
    adapter = centred(key_of[6], (DT, D), DT ** -0.5, 0.046875, ((0, 32), (1, 4)))
    w_gate = centred(key_of[7], (D, FF), D ** -0.5, 0.09375, ((0, 4), (1, 32)))
    w_up = centred(key_of[8], (D, FF), D ** -0.5, 0.09375, ((0, 4), (1, 32)))
    w_down = centred(key_of[9], (FF, D), FF ** -0.5, 0.046875, ((0, 32), (1, 4)))
    return {"teacher_states": teacher_states, "layer_map": layer_map, "token_order": token_order, "student_states": student_states, "teacher_gain": teacher_gain, "student_gain": student_gain, "adapter": adapter, "w_gate": w_gate, "w_up": w_up, "w_down": w_down}


eps = 1e-05

def tdot(left, right):
    return lax.dot_general(left, right, (((0,), (0,)), ((), ())), preferred_element_type=jnp.float32)

def reference(teacher_states, layer_map, token_order, student_states, teacher_gain, student_gain, adapter, w_gate, w_up, w_down):
    chosen = lax.dynamic_index_in_dim(teacher_states, layer_map[0].astype(jnp.int32), 0, keepdims=False).astype(jnp.float32)
    trs = lax.rsqrt(lax.optimization_barrier(jnp.mean(chosen * chosen, axis=1, keepdims=True)) + eps)
    teacher_normed = (chosen * trs * teacher_gain.astype(jnp.float32)).astype(jnp.bfloat16)
    ordered = jnp.take(teacher_normed, token_order.astype(jnp.int32), axis=0)
    target = jnp.dot(ordered, adapter, preferred_element_type=jnp.float32)
    xval = student_states.astype(jnp.float32)
    srs = lax.rsqrt(lax.optimization_barrier(jnp.mean(xval * xval, axis=1, keepdims=True)) + eps)
    student_normed = (xval * srs * student_gain.astype(jnp.float32)).astype(jnp.bfloat16)
    gate = jnp.dot(student_normed, w_gate, preferred_element_type=jnp.float32)
    up = jnp.dot(student_normed, w_up, preferred_element_type=jnp.float32)
    sig = jax.nn.sigmoid(gate)
    hidden = (gate * sig * up).astype(jnp.bfloat16)
    mlp = jnp.dot(hidden, w_down, preferred_element_type=jnp.float32)
    diff = xval + mlp - target
    grad_out = (diff * (2.0 / TOKENS)).astype(jnp.bfloat16)
    grad_down = tdot(hidden, grad_out)
    grad_adapter = -tdot(ordered, grad_out)
    grad_hidden = lax.dot_general(grad_out, w_down, (((1,), (1,)), ((), ())), preferred_element_type=jnp.float32)
    grad_gate_pre = (grad_hidden * up * sig * (1.0 + gate * (1.0 - sig))).astype(jnp.bfloat16)
    grad_up_pre = (grad_hidden * gate * sig).astype(jnp.bfloat16)
    grad_gate = tdot(student_normed, grad_gate_pre)
    grad_up = tdot(student_normed, grad_up_pre)
    return (grad_gate, grad_up, grad_down, grad_adapter)
```

```python
import jax
import jax.numpy as jnp
from jax import lax
from jax.sharding import Mesh, PartitionSpec as P

DT = 16384
D = 4096
TOKENS = 2048
EPS = 1e-05
CHUNKS = 2
SIZES = {"x": 4, "zl": 2, "y": 4, "zh": 2, "c": 2}
F32 = jnp.float32
BF16 = jnp.bfloat16


def shift(v, axis, by):
    n = SIZES[axis]
    return lax.ppermute(v, axis, [(i, (i + by) % n) for i in range(n)])


def pieces(v, axis):
    return [v] + [shift(v, axis, d) for d in range(1, SIZES[axis])]


def total(v, axis):
    parts = pieces(v, axis)
    out = parts[0]
    for p in parts[1:]:
        out = out + p
    return out


def dot(a, b):
    return jnp.dot(a, b, preferred_element_type=F32)


def tdot(left, right):
    return lax.dot_general(left, right, (((0,), (0,)), ((), ())), preferred_element_type=F32)


def gather_rows(v):
    v = jnp.concatenate(pieces(v, "zl"), axis=0)
    n, cols = v.shape
    half = cols // 2
    left, right = v[:, :half], v[:, half:]
    left = jnp.concatenate(pieces(left, "y"), axis=0)
    right = jnp.concatenate(pieces(right, "x"), axis=0)
    left = jnp.concatenate(pieces(left, "x"), axis=0)
    right = jnp.stack(pieces(right, "y"), axis=0).reshape(4, 4, n, half)
    right = right.transpose(1, 0, 2, 3).reshape(16 * n, half)
    return jnp.concatenate([left, right], axis=1)


def add_up(blocks):
    out = blocks[0].astype(F32)
    for b in blocks[1:]:
        out = out + b.astype(F32)
    return out


def scatter_rows(v):
    rows, cols = v.shape
    n, half = rows // 16, cols // 2
    v = v.reshape(4, 4, n, cols)
    left, right = v[..., :half], v[..., half:]
    left = add_up([shift(left[d], "x", -d) if d else left[d] for d in range(4)]).astype(BF16)
    right = add_up([shift(right[:, d], "y", -d) if d else right[:, d] for d in range(4)]).astype(BF16)
    left = add_up([shift(left[d], "y", -d) if d else left[d] for d in range(4)])
    right = add_up([shift(right[d], "x", -d) if d else right[d] for d in range(4)])
    v = jnp.concatenate([left, right], axis=1)
    m = n // 2
    return v[:m] + shift(v[m:].astype(BF16), "zl", 1).astype(F32)


def own_half(v, axis, other=False):
    half = v.shape[0] // 2
    at = lax.axis_index(axis)
    if other:
        at = 1 - at
    return lax.dynamic_slice_in_dim(v, at * half, half, axis=0)


def scatter_tensor(rows, fn):
    theirs = fn(own_half(rows, "c", True)).astype(BF16)
    got = shift(theirs, "c", 1)
    mine = fn(own_half(rows, "c")) + got.astype(F32)
    got = shift(own_half(mine, "zh", True).astype(BF16), "zh", 1)
    return own_half(mine, "zh") + got.astype(F32)


def gather_half(v, axis):
    other = shift(v, axis, 1)
    first = lax.axis_index(axis) == 0
    return jnp.concatenate([jnp.where(first, v, other), jnp.where(first, other, v)], axis=0)


def gather_tensor(v):
    return gather_half(gather_half(v, "zh"), "c")


def relative_tokens(token_order):
    order = token_order.reshape(4, 2, 4, CHUNKS, TOKENS // 32 // CHUNKS)
    for dim, name in ((0, "x"), (1, "zl"), (2, "y")):
        n = SIZES[name]
        order = jnp.flip(order, axis=dim)
        order = jnp.concatenate([order, order], axis=dim)
        order = lax.dynamic_slice_in_dim(order, n - 1 - lax.axis_index(name), n, axis=dim)
    return order.transpose(3, 0, 2, 1, 4).reshape(CHUNKS, TOKENS // CHUNKS)


def body(
    teacher_states,
    layer_map,
    token_order,
    student_states,
    teacher_gain,
    student_gain,
    adapter,
    w_gate,
    w_up,
    w_down,
):
    xval = student_states.astype(F32)
    student_sq = jnp.sum(xval * xval, axis=1)
    student_sq = total(total(student_sq, "c"), "zh")
    srs = lax.rsqrt(student_sq / D + EPS)
    student_normed = (xval * srs[:, None] * student_gain.astype(F32)).astype(BF16)

    chosen = lax.dynamic_index_in_dim(teacher_states, layer_map[0], 0, keepdims=False).astype(F32)
    teacher_sq = jnp.sum(chosen * chosen, axis=1)
    teacher_sq = total(total(total(teacher_sq, "zl"), "x"), "y")
    trs = lax.rsqrt(teacher_sq / DT + EPS)
    teacher_normed = (chosen * trs[:, None] * teacher_gain.astype(F32)).astype(BF16)
    order = relative_tokens(token_order)

    w_both = jnp.concatenate([w_gate, w_up], axis=1)
    ff = w_gate.shape[1]
    rows = student_states.shape[0] // CHUNKS

    student = [gather_rows(student_normed[k * rows : (k + 1) * rows]) for k in range(CHUNKS)]
    teacher_all = gather_half(gather_half(teacher_normed, "c"), "zh")
    ordered = [jnp.take(teacher_all, order[k], axis=0) for k in range(CHUNKS)]
    target = [dot(ordered[k], adapter) for k in range(CHUNKS)]

    grads = None
    for k in range(CHUNKS):
        both = scatter_tensor(student[k], lambda v: dot(v, w_both))
        gate, up = both[:, :ff], both[:, ff:]
        sig = jax.nn.sigmoid(gate)
        hidden = gather_tensor((gate * sig * up).astype(BF16))
        part = (dot(hidden, w_down) - target[k]).astype(BF16)
        diff = xval[k * rows : (k + 1) * rows] + scatter_rows(part)
        grad_out = gather_rows((diff * (2.0 / TOKENS)).astype(BF16))
        grad_hidden = scatter_tensor(
            grad_out,
            lambda v: lax.dot_general(v, w_down, (((1,), (1,)), ((), ())), preferred_element_type=F32),
        )
        gate_pre = grad_hidden * up * sig * (1.0 + gate * (1.0 - sig))
        up_pre = grad_hidden * gate * sig
        pre = gather_tensor(jnp.concatenate([gate_pre, up_pre], axis=1).astype(BF16))
        new = (
            tdot(student[k], pre[:, :ff]),
            tdot(student[k], pre[:, ff:]),
            tdot(hidden, grad_out),
            -tdot(ordered[k], grad_out),
        )
        grads = new if grads is None else tuple(a + b for a, b in zip(grads, new))
    return grads


def solution(mesh):
    fine = Mesh(mesh.devices.reshape(4, 2, 4, 2, 2), tuple(SIZES))
    dp, tensor = ("x", "zl", "y"), ("zh", "c")
    in_specs = (
        P(None, tensor, dp),
        P(),
        P(),
        P(dp, tensor),
        P(dp),
        P(tensor),
        P(dp, tensor),
        P(tensor, dp),
        P(tensor, dp),
        P(dp, tensor),
    )
    out_specs = (P(tensor, dp), P(tensor, dp), P(dp, tensor), P(dp, tensor))
    return jax.shard_map(body, mesh=fine, in_specs=in_specs, out_specs=out_specs, check_vma=False)
```

```python
import jax
import jax.numpy as jnp
from jax import lax
from jax.sharding import Mesh, PartitionSpec as P

DT = 16384
D = 4096
TOKENS = 2048
EPS = 1e-05
SIZES = {"x": 4, "zl": 2, "y": 4, "zh": 2, "c": 2}
F32 = jnp.float32
BF16 = jnp.bfloat16
fence = lax.optimization_barrier


def swap(v, axis):
    return lax.ppermute(v, axis, [(0, 1), (1, 0)])


def turn(v, way, by):
    pairs = []
    for x in range(4):
        for y in range(4):
            for c in range(2):
                to = ((x + by) % 4, y) if c == way else (x, (y + by) % 4)
                pairs.append(((x * 4 + y) * 2 + c, (to[0] * 4 + to[1]) * 2 + c))
    return lax.ppermute(v, ("x", "y", "c"), pairs)


def on_core(first, second):
    return jnp.where(lax.axis_index("c") == 0, first, second)


def dot(a, b):
    return jnp.dot(a, b, preferred_element_type=F32)


def tdot(left, right):
    return lax.dot_general(left, right, (((0,), (0,)), ((), ())), preferred_element_type=F32)


def gather_rows(v):
    quarters, n, cols = v.shape
    v = jnp.concatenate([v, swap(v, "zl")], axis=1)
    v = jnp.stack([v] + [turn(v, 1, d) for d in (1, 2, 3)], axis=1)
    blocks = [v] + [turn(v, 0, d) for d in (1, 2, 3)]
    v = on_core(jnp.stack(blocks, axis=1), jnp.stack(blocks, axis=2))
    return v.reshape(quarters * 32 * n, cols)


def add_up(blocks):
    out = blocks[0].astype(F32)
    for b in blocks[1:]:
        out = out + b.astype(F32)
    return out


def scatter_rows(v):
    rows, cols = v.shape
    v = v.reshape(4, 4, 4, rows // 64, cols)
    blocks = [on_core(v[:, d], v[:, :, d]) for d in range(4)]
    v = add_up([blocks[0]] + [turn(blocks[d], 0, -d) for d in (1, 2, 3)]).astype(BF16)
    v = add_up([v[:, 0]] + [turn(v[:, d], 1, -d) for d in (1, 2, 3)])
    n = v.shape[1] // 2
    return v[:, :n] + swap(v[:, n:].astype(BF16), "zl").astype(F32)


def scatter_tensor(rows, fn):
    n = rows.shape[0] // 4
    got = swap(fn(rows[3 * n :]).astype(BF16), "c")
    send = (fn(rows[2 * n : 3 * n]) + got.astype(F32)).astype(BF16)
    send, rows = fence((send, rows))
    far = swap(send, "zh")
    near = swap(fn(rows[n : 2 * n]).astype(BF16), "c")
    return fn(rows[:n]) + near.astype(F32) + far.astype(F32)


def quarters_first(v, at):
    for axis, name in ((at, "zh"), (at + 1, "c")):
        v = jnp.where(lax.axis_index(name) == 1, jnp.flip(v, axis=axis), v)
    return v


def relative_tokens(token_order):
    quarter = TOKENS // 4
    own = lax.axis_index("zh") * 2 + lax.axis_index("c")
    token_order = ((token_order // quarter) ^ own) * quarter + token_order % quarter
    order = token_order.reshape(4, 2, 4, 2, 2, TOKENS // 128)
    for dim, name in ((0, "x"), (1, "zl"), (2, "y")):
        n = SIZES[name]
        order = jnp.flip(order, axis=dim)
        order = jnp.concatenate([order, order], axis=dim)
        order = lax.dynamic_slice_in_dim(order, n - 1 - lax.axis_index(name), n, axis=dim)
    return quarters_first(order, 3).transpose(3, 4, 0, 2, 1, 5).reshape(TOKENS)


def body(
    teacher_states,
    layer_map,
    token_order,
    student_states,
    teacher_gain,
    student_gain,
    adapter,
    w_gate,
    w_up,
    w_down,
):
    ff = w_gate.shape[1]
    rows, cols = student_states.shape
    raw = student_states.astype(F32)
    student_sq = jnp.sum(raw * raw, axis=1)
    student_sq = student_sq + swap(student_sq, "c")
    student_sq = student_sq + swap(student_sq, "zh")
    srs = lax.rsqrt(student_sq / D + EPS)
    xval = quarters_first(student_states.reshape(2, 2, rows // 4, cols), 0).reshape(4, rows // 4, cols).astype(F32)
    srs = quarters_first(srs.reshape(2, 2, rows // 4), 0).reshape(4, rows // 4)
    student_normed = (xval * srs[..., None] * student_gain.astype(F32)).astype(BF16)

    chosen = lax.dynamic_index_in_dim(teacher_states, layer_map[0], 0, keepdims=False)
    chosen, student_normed = fence((chosen, student_normed))
    student = gather_rows(student_normed)
    w_both = jnp.concatenate([w_gate, w_up], axis=1)
    order = relative_tokens(token_order)
    chosen_f32 = chosen.astype(F32)
    teacher_sq = jnp.sum(chosen_f32 * chosen_f32, axis=1)
    every = ("x", "zl", "y", "zh", "c")
    teacher_sq = jnp.broadcast_to(teacher_sq.reshape(1, 4, 128), (128, 4, 128))
    teacher_sq = lax.all_to_all(teacher_sq, every, 0, 0, tiled=True)
    teacher_sq = jnp.sum(teacher_sq.reshape(32, 2, 2, -1), axis=0)
    trs = lax.rsqrt(quarters_first(teacher_sq, 0).reshape(-1) / DT + EPS)
    beyond = swap(chosen, "zh")
    teacher_all = jnp.concatenate([chosen, swap(chosen, "c"), beyond, swap(beyond, "c")], axis=0)
    student, teacher_all, trs, w_both, order = fence((student, teacher_all, trs, w_both, order))

    both = scatter_tensor(student, lambda v: dot(v, w_both))
    teacher_normed = (teacher_all.astype(F32) * trs[:, None] * teacher_gain.astype(F32)).astype(BF16)
    ordered = jnp.take(teacher_normed, order, axis=0)
    target = dot(ordered, adapter)
    both, ordered, target = fence((both, ordered, target))
    gate, up = both[:, :ff], both[:, ff:]
    sig = jax.nn.sigmoid(gate)
    hidden = (gate * sig * up).astype(BF16)
    beyond = swap(hidden, "zh")
    hidden = jnp.concatenate([hidden, swap(hidden, "c"), beyond, swap(beyond, "c")], axis=0)
    part = (dot(hidden, w_down) - target).astype(BF16)
    diff = xval + scatter_rows(part)
    grad_out = gather_rows((diff * (2.0 / TOKENS)).astype(BF16))

    grad_hidden = scatter_tensor(
        grad_out,
        lambda v: lax.dot_general(v, w_down, (((1,), (1,)), ((), ())), preferred_element_type=F32),
    )
    gate_pre = grad_hidden * up * sig * (1.0 + gate * (1.0 - sig))
    up_pre = grad_hidden * gate * sig
    pre = jnp.concatenate([gate_pre, up_pre], axis=1).astype(BF16)
    beyond = swap(pre, "zh")
    pre = jnp.concatenate([pre, swap(pre, "c")], axis=0)
    half = TOKENS // 2
    first = (
        tdot(student[:half], pre[:, :ff]),
        tdot(student[:half], pre[:, ff:]),
        tdot(hidden, grad_out),
        -tdot(ordered, grad_out),
    )
    beyond, first = fence((beyond, first))
    pre = jnp.concatenate([beyond, swap(beyond, "c")], axis=0)
    return (
        first[0] + tdot(student[half:], pre[:, :ff]),
        first[1] + tdot(student[half:], pre[:, ff:]),
        first[2],
        first[3],
    )


def solution(mesh):
    fine = Mesh(mesh.devices.reshape(4, 2, 4, 2, 2), tuple(SIZES))
    dp, tensor = ("x", "zl", "y"), ("zh", "c")
    in_specs = (
        P(None, tensor, dp),
        P(),
        P(),
        P(dp, tensor),
        P(dp),
        P(tensor),
        P(dp, tensor),
        P(tensor, dp),
        P(tensor, dp),
        P(dp, tensor),
    )
    out_specs = (P(tensor, dp), P(tensor, dp), P(dp, tensor), P(dp, tensor))
    return jax.shard_map(body, mesh=fine, in_specs=in_specs, out_specs=out_specs, check_vma=False)
```

```python
import jax
import jax.numpy as jnp
from jax import lax
from jax.sharding import Mesh, PartitionSpec as P

DT = 16384
D = 4096
TOKENS = 2048
EPS = 1e-05
SIZES = {"x": 4, "zl": 2, "y": 4, "zh": 2, "c": 2}
F32 = jnp.float32
BF16 = jnp.bfloat16
fence = lax.optimization_barrier


def swap(v, axis):
    return lax.ppermute(v, axis, [(0, 1), (1, 0)])


def turn(v, way, by):
    pairs = []
    for x in range(4):
        for y in range(4):
            for c in range(2):
                to = ((x + by) % 4, y) if c == way else (x, (y + by) % 4)
                pairs.append(((x * 4 + y) * 2 + c, (to[0] * 4 + to[1]) * 2 + c))
    return lax.ppermute(v, ("x", "y", "c"), pairs)


def on_core(first, second):
    return jnp.where(lax.axis_index("c") == 0, first, second)


def dot(a, b):
    return jnp.dot(a, b, preferred_element_type=F32)


def tdot(left, right):
    return lax.dot_general(left, right, (((0,), (0,)), ((), ())), preferred_element_type=F32)


def gather_near(v, beside):
    v, beside = fence((v, swap(beside, "c")))
    return jnp.stack([v] + [turn(v, 1, d) for d in (1, 2, 3)], axis=1), beside


def gather_far(v):
    quarters, _, n, cols = v.shape
    blocks = [v] + [turn(v, 0, d) for d in (1, 2, 3)]
    v = on_core(jnp.stack(blocks, axis=1), jnp.stack(blocks, axis=2))
    return v.reshape(quarters * 16 * n, cols)


def add_up(blocks):
    out = blocks[0].astype(F32)
    for b in blocks[1:]:
        out = out + b.astype(F32)
    return out


def scatter_far(v):
    rows, cols = v.shape
    v = v.reshape(2, 4, 4, rows // 32, cols)
    blocks = [on_core(v[:, d], v[:, :, d]) for d in range(4)]
    return add_up([blocks[0]] + [turn(blocks[d], 0, -d) for d in (1, 2, 3)]).astype(BF16)


def scatter_near(v):
    v = add_up([v[:, 0]] + [turn(v[:, d], 1, -d) for d in (1, 2, 3)]).astype(BF16)
    n = v.shape[1] // 2
    other = swap(v, "zl").astype(F32)
    return v.astype(F32) + jnp.concatenate([other[:, n:], other[:, :n]], axis=1)


def send_far(rows, fn, beside):
    n = rows.shape[0] // 2
    got = swap(fn(rows[n:]).astype(BF16), "c")
    send = (fn(rows[:n]) + got.astype(F32)).astype(BF16)
    send, beside = fence((send, beside))
    return swap(send, "zh"), beside


def sum_near(rows, fn):
    n = rows.shape[0] // 2
    got = swap(fn(rows[n:]).astype(BF16), "c")
    return fn(rows[:n]) + got.astype(F32)


def quarters_first(v, at):
    for axis, name in ((at, "zh"), (at + 1, "c")):
        v = jnp.where(lax.axis_index(name) == 1, jnp.flip(v, axis=axis), v)
    return v


def relative_tokens(token_order):
    quarter = TOKENS // 4
    own = lax.axis_index("zh") * 2 + lax.axis_index("c")
    token_order = ((token_order // quarter) ^ own) * quarter + token_order % quarter
    order = token_order.reshape(4, 2, 4, 2, 2, TOKENS // 128)
    for dim, name in ((0, "x"), (1, "zl"), (2, "y")):
        n = SIZES[name]
        order = jnp.flip(order, axis=dim)
        order = jnp.concatenate([order, order], axis=dim)
        order = lax.dynamic_slice_in_dim(order, n - 1 - lax.axis_index(name), n, axis=dim)
    return quarters_first(order, 3).transpose(3, 4, 0, 2, 1, 5).reshape(TOKENS)


def body(
    teacher_states,
    layer_map,
    token_order,
    student_states,
    teacher_gain,
    student_gain,
    adapter,
    w_gate,
    w_up,
    w_down,
):
    ff = w_gate.shape[1]
    rows, cols = student_states.shape
    raw = student_states.astype(F32)
    student_sq = jnp.sum(raw * raw, axis=1)
    student_sq = student_sq + swap(student_sq, "c")
    student_sq = student_sq + swap(student_sq, "zh")
    srs = lax.rsqrt(student_sq / D + EPS)
    states = quarters_first(student_states.reshape(2, 2, rows // 4, cols), 0).reshape(4, rows // 4, cols)
    xval = states.astype(F32)
    srs = quarters_first(srs.reshape(2, 2, rows // 4), 0).reshape(4, rows // 4)
    student_normed = (xval * srs[..., None] * student_gain.astype(F32)).astype(BF16)

    xpair = jnp.concatenate([xval, swap(states, "zl").astype(F32)], axis=1)
    normed = jnp.concatenate([student_normed, swap(student_normed, "zl")], axis=1)
    near, srs = gather_near(normed, srs)
    chosen = lax.dynamic_index_in_dim(teacher_states, layer_map[0], 0, keepdims=False)
    chosen, near = fence((chosen, near))
    student_hi = gather_far(near[2:])
    w_both = jnp.concatenate([w_gate, w_up], axis=1)
    order = relative_tokens(token_order)
    chosen_f32 = chosen.astype(F32)
    teacher_sq = jnp.sum(chosen_f32 * chosen_f32, axis=1)
    beyond = swap(chosen, "zh")
    student_hi, near, w_both, order, teacher_sq = fence((student_hi, near, w_both, order, teacher_sq))

    def to_ff(v):
        return dot(v, w_both)

    student_lo = gather_far(near[:2])
    far, teacher_sq = send_far(student_hi, to_ff, teacher_sq)
    every = ("x", "zl", "y", "zh", "c")
    teacher_sq = jnp.broadcast_to(teacher_sq.reshape(1, 4, 128), (128, 4, 128))
    teacher_sq = lax.all_to_all(teacher_sq, every, 0, 0, tiled=True)
    teacher_sq = jnp.sum(teacher_sq.reshape(32, 2, 2, -1), axis=0)
    trs = lax.rsqrt(quarters_first(teacher_sq, 0).reshape(-1) / DT + EPS)
    teacher_all = jnp.concatenate([chosen, swap(chosen, "c"), beyond, swap(beyond, "c")], axis=0)
    both = sum_near(student_lo, to_ff)
    teacher_normed = (teacher_all.astype(F32) * trs[:, None] * teacher_gain.astype(F32)).astype(BF16)
    ordered = jnp.take(teacher_normed, order, axis=0)
    both, far, ordered = fence((both, far, ordered))
    target = dot(ordered, adapter)
    both = both + far.astype(F32)
    gate, up = both[:, :ff], both[:, ff:]
    sig = jax.nn.sigmoid(gate)
    hidden = (gate * sig * up).astype(BF16)
    half = TOKENS // 2
    beyond = swap(hidden, "zh")
    hidden_lo = jnp.concatenate([hidden, swap(hidden, "c")], axis=0)
    sum_lo = scatter_far((dot(hidden_lo, w_down) - target[:half]).astype(BF16))
    hidden_hi = jnp.concatenate([beyond, swap(beyond, "c")], axis=0)
    sum_hi = scatter_far((dot(hidden_hi, w_down) - target[half:]).astype(BF16))
    diff = xpair + scatter_near(jnp.concatenate([sum_lo, sum_hi], axis=0))
    grad_out = (diff * (2.0 / TOKENS)).astype(BF16)
    near, _ = gather_near(grad_out, srs)
    grad_out_hi = gather_far(near[2:])
    grad_out_hi, near = fence((grad_out_hi, near))

    def to_hidden(v):
        return lax.dot_general(v, w_down, (((1,), (1,)), ((), ())), preferred_element_type=F32)

    grad_out_lo = gather_far(near[:2])
    far, _ = send_far(grad_out_hi, to_hidden, srs)
    grad_hidden = sum_near(grad_out_lo, to_hidden)
    grad_out = jnp.concatenate([grad_out_lo, grad_out_hi], axis=0)
    hidden = jnp.concatenate([hidden_lo, hidden_hi], axis=0)
    grad_down = tdot(hidden, grad_out)
    grad_adapter = -tdot(ordered, grad_out)
    grad_hidden, far, grad_down, grad_adapter = fence((grad_hidden, far, grad_down, grad_adapter))
    grad_hidden = grad_hidden + far.astype(F32)
    gate_pre = grad_hidden * up * sig * (1.0 + gate * (1.0 - sig))
    up_pre = grad_hidden * gate * sig
    pre = jnp.concatenate([gate_pre, up_pre], axis=1).astype(BF16)
    beyond = swap(pre, "zh")
    pre = jnp.concatenate([pre, swap(pre, "c")], axis=0)
    first = (tdot(student_lo, pre[:, :ff]), tdot(student_lo, pre[:, ff:]))
    beyond, first = fence((beyond, first))
    pre = jnp.concatenate([beyond, swap(beyond, "c")], axis=0)
    return (
        first[0] + tdot(student_hi, pre[:, :ff]),
        first[1] + tdot(student_hi, pre[:, ff:]),
        grad_down,
        grad_adapter,
    )


def solution(mesh):
    fine = Mesh(mesh.devices.reshape(4, 2, 4, 2, 2), tuple(SIZES))
    dp, tensor = ("x", "zl", "y"), ("zh", "c")
    in_specs = (
        P(None, tensor, dp),
        P(),
        P(),
        P(dp, tensor),
        P(dp),
        P(tensor),
        P(dp, tensor),
        P(tensor, dp),
        P(tensor, dp),
        P(dp, tensor),
    )
    out_specs = (P(tensor, dp), P(tensor, dp), P(dp, tensor), P(dp, tensor))
    return jax.shard_map(body, mesh=fine, in_specs=in_specs, out_specs=out_specs, check_vma=False)
```

```python
import jax
import jax.numpy as jnp
from jax import lax
from jax.sharding import Mesh, PartitionSpec as P

DT = 16384
D = 4096
TOKENS = 2048
EPS = 1e-05
SIZES = {"x": 4, "zl": 2, "y": 4, "zh": 2, "c": 2}
F32 = jnp.float32
BF16 = jnp.bfloat16
fence = lax.optimization_barrier


def swap(v, axis):
    return lax.ppermute(v, axis, [(0, 1), (1, 0)])


def turn(v, way, by):
    pairs = []
    for x in range(4):
        for y in range(4):
            for c in range(2):
                to = ((x + by) % 4, y) if c == way else (x, (y + by) % 4)
                pairs.append(((x * 4 + y) * 2 + c, (to[0] * 4 + to[1]) * 2 + c))
    return lax.ppermute(v, ("x", "y", "c"), pairs)


def on_core(first, second):
    return jnp.where(lax.axis_index("c") == 0, first, second)


def dot(a, b):
    return jnp.dot(a, b, preferred_element_type=F32)


def tdot(left, right):
    return lax.dot_general(left, right, (((0,), (0,)), ((), ())), preferred_element_type=F32)


def gather_near(v, beside):
    v, beside = fence((v, swap(beside, "c")))
    return jnp.stack([v] + [turn(v, 1, d) for d in (1, 2, 3)], axis=1), beside


def gather_far(v):
    return far_rows(v, far_blocks(v))


def far_blocks(v):
    return [turn(v, 0, d) for d in (1, 2, 3)]


def far_rows(v, others):
    quarters, _, n, cols = v.shape
    blocks = [v] + others
    v = on_core(jnp.stack(blocks, axis=1), jnp.stack(blocks, axis=2))
    return v.reshape(quarters * 16 * n, cols)


def add_up(blocks):
    out = blocks[0].astype(F32)
    for b in blocks[1:]:
        out = out + b.astype(F32)
    return out


def scatter_far(v):
    rows, cols = v.shape
    v = v.reshape(2, 4, 4, rows // 32, cols)
    blocks = [on_core(v[:, d], v[:, :, d]) for d in range(4)]
    return add_up([blocks[0]] + [turn(blocks[d], 0, -d) for d in (1, 2, 3)]).astype(BF16)


def scatter_near(v):
    v = add_up([v[:, 0]] + [turn(v[:, d], 1, -d) for d in (1, 2, 3)]).astype(BF16)
    n = v.shape[1] // 2
    other = swap(v, "zl").astype(F32)
    return v.astype(F32) + jnp.concatenate([other[:, n:], other[:, :n]], axis=1)


def send_far(rows, fn, beside):
    n = rows.shape[0] // 2
    got = swap(fn(rows[n:]).astype(BF16), "c")
    send = (fn(rows[:n]) + got.astype(F32)).astype(BF16)
    send, beside = fence((send, beside))
    return swap(send, "zh"), beside


def sum_near(rows, fn):
    n = rows.shape[0] // 2
    got = swap(fn(rows[n:]).astype(BF16), "c")
    return fn(rows[:n]) + got.astype(F32)


def quarters_first(v, at):
    for axis, name in ((at, "zh"), (at + 1, "c")):
        v = jnp.where(lax.axis_index(name) == 1, jnp.flip(v, axis=axis), v)
    return v


def relative_tokens(token_order):
    quarter = TOKENS // 4
    own = lax.axis_index("zh") * 2 + lax.axis_index("c")
    token_order = ((token_order // quarter) ^ own) * quarter + token_order % quarter
    order = token_order.reshape(4, 2, 4, 2, 2, TOKENS // 128)
    for dim, name in ((0, "x"), (1, "zl"), (2, "y")):
        n = SIZES[name]
        order = jnp.flip(order, axis=dim)
        order = jnp.concatenate([order, order], axis=dim)
        order = lax.dynamic_slice_in_dim(order, n - 1 - lax.axis_index(name), n, axis=dim)
    return quarters_first(order, 3).transpose(3, 4, 0, 2, 1, 5).reshape(TOKENS)


def body(
    teacher_states,
    layer_map,
    token_order,
    student_states,
    teacher_gain,
    student_gain,
    adapter,
    w_gate,
    w_up,
    w_down,
):
    ff = w_gate.shape[1]
    rows, cols = student_states.shape
    raw = student_states.astype(F32)
    student_sq = jnp.sum(raw * raw, axis=1)
    student_sq = student_sq + swap(student_sq, "c")
    student_sq = student_sq + swap(student_sq, "zh")
    srs = lax.rsqrt(student_sq / D + EPS)
    states = quarters_first(student_states.reshape(2, 2, rows // 4, cols), 0).reshape(4, rows // 4, cols)
    xval = states.astype(F32)
    srs = quarters_first(srs.reshape(2, 2, rows // 4), 0).reshape(4, rows // 4)
    student_normed = (xval * srs[..., None] * student_gain.astype(F32)).astype(BF16)

    xpair = jnp.concatenate([xval, swap(states, "zl").astype(F32)], axis=1)
    normed = jnp.concatenate([student_normed, swap(student_normed, "zl")], axis=1)
    near, srs = gather_near(normed, srs)
    chosen = lax.dynamic_index_in_dim(teacher_states, layer_map[0], 0, keepdims=False)
    chosen, near = fence((chosen, near))
    student_hi = gather_far(near[2:])
    w_both = jnp.concatenate([w_gate, w_up], axis=1)
    order = relative_tokens(token_order)
    chosen_f32 = chosen.astype(F32)
    teacher_sq = jnp.sum(chosen_f32 * chosen_f32, axis=1)
    beyond = swap(chosen, "zh")
    beside = swap(chosen, "c")
    student_hi, near, w_both, order, teacher_sq = fence((student_hi, near, w_both, order, teacher_sq))

    def to_ff(v):
        return dot(v, w_both)

    others = far_blocks(near[:2])
    far, (mine, teacher_sq) = send_far(student_hi, to_ff, (near[:2], teacher_sq))
    student_lo = far_rows(mine, others)
    every = ("x", "zl", "y", "zh", "c")
    teacher_sq = jnp.broadcast_to(teacher_sq.reshape(1, 4, 128), (128, 4, 128))
    teacher_sq = lax.all_to_all(teacher_sq, every, 0, 0, tiled=True)
    teacher_sq = jnp.sum(teacher_sq.reshape(32, 2, 2, -1), axis=0)
    trs = lax.rsqrt(quarters_first(teacher_sq, 0).reshape(-1) / DT + EPS)
    teacher_all = jnp.concatenate([chosen, beside, beyond, swap(beyond, "c")], axis=0)
    both = sum_near(student_lo, to_ff)
    teacher_normed = (teacher_all.astype(F32) * trs[:, None] * teacher_gain.astype(F32)).astype(BF16)
    ordered = jnp.take(teacher_normed, order, axis=0)
    both, far, ordered = fence((both, far, ordered))
    target = dot(ordered, adapter)
    both = both + far.astype(F32)
    gate, up = both[:, :ff], both[:, ff:]
    sig = jax.nn.sigmoid(gate)
    hidden = (gate * sig * up).astype(BF16)
    half = TOKENS // 2
    beyond = swap(hidden, "zh")
    hidden_lo = jnp.concatenate([hidden, swap(hidden, "c")], axis=0)
    sum_lo = scatter_far((dot(hidden_lo, w_down) - target[:half]).astype(BF16))
    hidden_hi = jnp.concatenate([beyond, swap(beyond, "c")], axis=0)
    sum_hi = scatter_far((dot(hidden_hi, w_down) - target[half:]).astype(BF16))
    diff = xpair + scatter_near(jnp.concatenate([sum_lo, sum_hi], axis=0))
    grad_out = (diff * (2.0 / TOKENS)).astype(BF16)
    near, _ = gather_near(grad_out, srs)
    grad_out_hi = gather_far(near[2:])
    grad_out_hi, near = fence((grad_out_hi, near))

    def to_hidden(v):
        return lax.dot_general(v, w_down, (((1,), (1,)), ((), ())), preferred_element_type=F32)

    others = far_blocks(near[:2])
    far, mine = send_far(grad_out_hi, to_hidden, near[:2])
    grad_out_lo = far_rows(mine, others)
    grad_hidden = sum_near(grad_out_lo, to_hidden)
    grad_hidden = grad_hidden + far.astype(F32)
    gate_pre = grad_hidden * up * sig * (1.0 + gate * (1.0 - sig))
    up_pre = grad_hidden * gate * sig
    pre = jnp.concatenate([gate_pre, up_pre], axis=1).astype(BF16)
    beyond = swap(pre, "zh")
    other, grad_out_lo = fence((swap(pre, "c"), grad_out_lo))
    pre = jnp.concatenate([pre, other], axis=0)
    grad_out = jnp.concatenate([grad_out_lo, grad_out_hi], axis=0)
    hidden = jnp.concatenate([hidden_lo, hidden_hi], axis=0)
    grad_down = tdot(hidden, grad_out)
    grad_adapter = -tdot(ordered, grad_out)
    first = (tdot(student_lo, pre[:, :ff]), tdot(student_lo, pre[:, ff:]), grad_down, grad_adapter)
    beyond, first = fence((beyond, first))
    pre = jnp.concatenate([beyond, swap(beyond, "c")], axis=0)
    return (
        first[0] + tdot(student_hi, pre[:, :ff]),
        first[1] + tdot(student_hi, pre[:, ff:]),
        first[2],
        first[3],
    )


def solution(mesh):
    fine = Mesh(mesh.devices.reshape(4, 2, 4, 2, 2), tuple(SIZES))
    dp, tensor = ("x", "zl", "y"), ("zh", "c")
    in_specs = (
        P(None, tensor, dp),
        P(),
        P(),
        P(dp, tensor),
        P(dp),
        P(tensor),
        P(dp, tensor),
        P(tensor, dp),
        P(tensor, dp),
        P(dp, tensor),
    )
    out_specs = (P(tensor, dp), P(tensor, dp), P(dp, tensor), P(dp, tensor))
    return jax.shard_map(body, mesh=fine, in_specs=in_specs, out_specs=out_specs, check_vma=False)
```

```python
import jax
import jax.numpy as jnp
from jax import lax
from jax.sharding import Mesh, PartitionSpec as P

DT = 16384
D = 4096
TOKENS = 2048
EPS = 1e-05
SIZES = {"x": 4, "zl": 2, "y": 4, "zh": 2, "c": 2}
F32 = jnp.float32
BF16 = jnp.bfloat16
fence = lax.optimization_barrier


def swap(v, axis):
    return lax.ppermute(v, axis, [(0, 1), (1, 0)])


def turn(v, way, by):
    pairs = []
    for x in range(4):
        for y in range(4):
            for c in range(2):
                to = ((x + by) % 4, y) if c == way else (x, (y + by) % 4)
                pairs.append(((x * 4 + y) * 2 + c, (to[0] * 4 + to[1]) * 2 + c))
    return lax.ppermute(v, ("x", "y", "c"), pairs)


def on_core(first, second):
    return jnp.where(lax.axis_index("c") == 0, first, second)


def dot(a, b):
    return jnp.dot(a, b, preferred_element_type=F32)


def tdot(left, right):
    return lax.dot_general(left, right, (((0,), (0,)), ((), ())), preferred_element_type=F32)


def gather_near(v, beside):
    v, beside = fence((v, swap(beside, "c")))
    return jnp.stack([v] + [turn(v, 1, d) for d in (1, 2, 3)], axis=1), beside


def gather_far(v):
    return far_rows(v, far_blocks(v))


def far_blocks(v):
    return [turn(v, 0, d) for d in (1, 2, 3)]


def far_rows(v, others):
    quarters, _, n, cols = v.shape
    blocks = [v] + others
    v = on_core(jnp.stack(blocks, axis=1), jnp.stack(blocks, axis=2))
    return v.reshape(quarters * 16 * n, cols)


def add_up(blocks):
    out = blocks[0].astype(F32)
    for b in blocks[1:]:
        out = out + b.astype(F32)
    return out


def scatter_far(v):
    rows, cols = v.shape
    v = v.reshape(2, 4, 4, rows // 32, cols)
    blocks = [on_core(v[:, d], v[:, :, d]) for d in range(4)]
    return add_up([blocks[0]] + [turn(blocks[d], 0, -d) for d in (1, 2, 3)]).astype(BF16)


def scatter_near(v):
    v = add_up([v[:, 0]] + [turn(v[:, d], 1, -d) for d in (1, 2, 3)]).astype(BF16)
    n = v.shape[1] // 2
    other = swap(v, "zl").astype(F32)
    return v.astype(F32) + jnp.concatenate([other[:, n:], other[:, :n]], axis=1)


def send_far(rows, fn, beside):
    n = rows.shape[0] // 2
    got = swap(fn(rows[n:]).astype(BF16), "c")
    send = (fn(rows[:n]) + got.astype(F32)).astype(BF16)
    send, beside = fence((send, beside))
    return swap(send, "zh"), beside


def sum_near(rows, fn):
    n = rows.shape[0] // 2
    got = swap(fn(rows[n:]).astype(BF16), "c")
    return fn(rows[:n]) + got.astype(F32)


def quarters_first(v, at):
    for axis, name in ((at, "zh"), (at + 1, "c")):
        v = jnp.where(lax.axis_index(name) == 1, jnp.flip(v, axis=axis), v)
    return v


def relative_tokens(token_order):
    quarter = TOKENS // 4
    own = lax.axis_index("zh") * 2 + lax.axis_index("c")
    token_order = ((token_order // quarter) ^ own) * quarter + token_order % quarter
    order = token_order.reshape(4, 2, 4, 2, 2, TOKENS // 128)
    for dim, name in ((0, "x"), (1, "zl"), (2, "y")):
        n = SIZES[name]
        order = jnp.flip(order, axis=dim)
        order = jnp.concatenate([order, order], axis=dim)
        order = lax.dynamic_slice_in_dim(order, n - 1 - lax.axis_index(name), n, axis=dim)
    return quarters_first(order, 3).transpose(3, 4, 0, 2, 1, 5).reshape(TOKENS)


def body(
    teacher_states,
    layer_map,
    token_order,
    student_states,
    teacher_gain,
    student_gain,
    adapter,
    w_gate,
    w_up,
    w_down,
):
    ff = w_gate.shape[1]
    rows, cols = student_states.shape
    raw = student_states.astype(F32)
    student_sq = jnp.sum(raw * raw, axis=1)
    student_sq = student_sq + swap(student_sq, "c")
    student_sq = student_sq + swap(student_sq, "zh")
    srs = lax.rsqrt(student_sq / D + EPS)
    states = quarters_first(student_states.reshape(2, 2, rows // 4, cols), 0).reshape(4, rows // 4, cols)
    xval = states.astype(F32)
    srs = quarters_first(srs.reshape(2, 2, rows // 4), 0).reshape(4, rows // 4)
    student_normed = (xval * srs[..., None] * student_gain.astype(F32)).astype(BF16)

    xpair = jnp.concatenate([xval, swap(states, "zl").astype(F32)], axis=1)
    normed = jnp.concatenate([student_normed, swap(student_normed, "zl")], axis=1)
    chosen = lax.dynamic_index_in_dim(teacher_states, layer_map[0], 0, keepdims=False)
    chosen, normed = fence((chosen, normed))
    near, srs = gather_near(normed, srs)
    student_hi = gather_far(near[2:])
    w_both = jnp.concatenate([w_gate, w_up], axis=1)
    order = relative_tokens(token_order)
    chosen_f32 = chosen.astype(F32)
    teacher_sq = jnp.sum(chosen_f32 * chosen_f32, axis=1)
    beyond = swap(chosen, "zh")
    beside = swap(chosen, "c")
    student_hi, near, w_both, order, teacher_sq, beyond, beside = fence(
        (student_hi, near, w_both, order, teacher_sq, beyond, beside)
    )

    def to_ff(v):
        return dot(v, w_both)

    others = far_blocks(near[:2])
    far, (mine, teacher_sq, beyond) = send_far(student_hi, to_ff, (near[:2], teacher_sq, beyond))
    student_lo = far_rows(mine, others)
    every = ("x", "zl", "y", "zh", "c")
    teacher_sq = jnp.broadcast_to(teacher_sq.reshape(1, 4, 128), (128, 4, 128))
    teacher_sq = lax.all_to_all(teacher_sq, every, 0, 0, tiled=True)
    teacher_sq = jnp.sum(teacher_sq.reshape(32, 2, 2, -1), axis=0)
    trs = lax.rsqrt(quarters_first(teacher_sq, 0).reshape(-1) / DT + EPS)
    teacher_all = jnp.concatenate([chosen, beside, beyond, swap(beyond, "c")], axis=0)
    both = sum_near(student_lo, to_ff)
    teacher_normed = (teacher_all.astype(F32) * trs[:, None] * teacher_gain.astype(F32)).astype(BF16)
    ordered = jnp.take(teacher_normed, order, axis=0)
    both, far, ordered = fence((both, far, ordered))
    target = dot(ordered, adapter)
    both = both + far.astype(F32)
    gate, up = both[:, :ff], both[:, ff:]
    sig = jax.nn.sigmoid(gate)
    hidden = (gate * sig * up).astype(BF16)
    half = TOKENS // 2
    beyond = swap(hidden, "zh")
    hidden_lo = jnp.concatenate([hidden, swap(hidden, "c")], axis=0)
    sum_lo = scatter_far((dot(hidden_lo, w_down) - target[:half]).astype(BF16))
    hidden_hi = jnp.concatenate([beyond, swap(beyond, "c")], axis=0)
    sum_hi = scatter_far((dot(hidden_hi, w_down) - target[half:]).astype(BF16))
    diff = xpair + scatter_near(jnp.concatenate([sum_lo, sum_hi], axis=0))
    grad_out = (diff * (2.0 / TOKENS)).astype(BF16)
    near, _ = gather_near(grad_out, srs)
    grad_out_hi = gather_far(near[2:])
    grad_out_hi, near = fence((grad_out_hi, near))

    def to_hidden(v):
        return lax.dot_general(v, w_down, (((1,), (1,)), ((), ())), preferred_element_type=F32)

    others = far_blocks(near[:2])
    far, mine = send_far(grad_out_hi, to_hidden, near[:2])
    grad_out_lo = far_rows(mine, others)
    grad_hidden = sum_near(grad_out_lo, to_hidden)
    grad_hidden = grad_hidden + far.astype(F32)
    gate_pre = grad_hidden * up * sig * (1.0 + gate * (1.0 - sig))
    up_pre = grad_hidden * gate * sig
    pre = jnp.concatenate([gate_pre, up_pre], axis=1).astype(BF16)
    beyond = swap(pre, "zh")
    other, grad_out_lo = fence((swap(pre, "c"), grad_out_lo))
    pre = jnp.concatenate([pre, other], axis=0)
    grad_out = jnp.concatenate([grad_out_lo, grad_out_hi], axis=0)
    hidden = jnp.concatenate([hidden_lo, hidden_hi], axis=0)
    grad_down = tdot(hidden, grad_out)
    grad_adapter = -tdot(ordered, grad_out)
    first = (tdot(student_lo, pre[:, :ff]), tdot(student_lo, pre[:, ff:]), grad_down, grad_adapter)
    beyond, first = fence((beyond, first))
    pre = jnp.concatenate([beyond, swap(beyond, "c")], axis=0)
    return (
        first[0] + tdot(student_hi, pre[:, :ff]),
        first[1] + tdot(student_hi, pre[:, ff:]),
        first[2],
        first[3],
    )


def solution(mesh):
    fine = Mesh(mesh.devices.reshape(4, 2, 4, 2, 2), tuple(SIZES))
    dp, tensor = ("x", "zl", "y"), ("zh", "c")
    in_specs = (
        P(None, tensor, dp),
        P(),
        P(),
        P(dp, tensor),
        P(dp),
        P(tensor),
        P(dp, tensor),
        P(tensor, dp),
        P(tensor, dp),
        P(dp, tensor),
    )
    out_specs = (P(tensor, dp), P(tensor, dp), P(dp, tensor), P(dp, tensor))
    return jax.shard_map(body, mesh=fine, in_specs=in_specs, out_specs=out_specs, check_vma=False)
```

```python
import jax
import jax.numpy as jnp
from jax import lax
from jax.sharding import Mesh, PartitionSpec as P

DT = 16384
D = 4096
TOKENS = 2048
EPS = 1e-05
SIZES = {"x": 4, "zl": 2, "y": 4, "zh": 2, "c": 2}
F32 = jnp.float32
BF16 = jnp.bfloat16
fence = lax.optimization_barrier


def swap(v, axis):
    return lax.ppermute(v, axis, [(0, 1), (1, 0)])


def turn(v, way, by):
    pairs = []
    for x in range(4):
        for y in range(4):
            for c in range(2):
                to = ((x + by) % 4, y) if c == way else (x, (y + by) % 4)
                pairs.append(((x * 4 + y) * 2 + c, (to[0] * 4 + to[1]) * 2 + c))
    return lax.ppermute(v, ("x", "y", "c"), pairs)


def on_core(first, second):
    return jnp.where(lax.axis_index("c") == 0, first, second)


def dot(a, b):
    return jnp.dot(a, b, preferred_element_type=F32)


def tdot(left, right):
    return lax.dot_general(left, right, (((0,), (0,)), ((), ())), preferred_element_type=F32)


def gather_near(v, beside):
    v, beside = fence((v, swap(beside, "c")))
    return jnp.stack([v] + [turn(v, 1, d) for d in (1, 2, 3)], axis=1), beside


def gather_far(v):
    return far_rows(v, far_blocks(v))


def far_blocks(v):
    return [turn(v, 0, d) for d in (1, 2, 3)]


def far_rows(v, others):
    quarters, _, n, cols = v.shape
    blocks = [v] + others
    v = on_core(jnp.stack(blocks, axis=1), jnp.stack(blocks, axis=2))
    return v.reshape(quarters * 16 * n, cols)


def add_up(blocks):
    out = blocks[0].astype(F32)
    for b in blocks[1:]:
        out = out + b.astype(F32)
    return out


def scatter_far(v):
    rows, cols = v.shape
    v = v.reshape(2, 4, 4, rows // 32, cols)
    blocks = [on_core(v[:, d], v[:, :, d]) for d in range(4)]
    return add_up([blocks[0]] + [turn(blocks[d], 0, -d) for d in (1, 2, 3)]).astype(BF16)


def scatter_near(v):
    v = add_up([v[:, 0]] + [turn(v[:, d], 1, -d) for d in (1, 2, 3)]).astype(BF16)
    n = v.shape[1] // 2
    other = swap(v, "zl").astype(F32)
    return v.astype(F32) + jnp.concatenate([other[:, n:], other[:, :n]], axis=1)


def send_far(rows, fn, beside):
    n = rows.shape[0] // 2
    got = swap(fn(rows[n:]).astype(BF16), "c")
    send = (fn(rows[:n]) + got.astype(F32)).astype(BF16)
    send, beside = fence((send, beside))
    return swap(send, "zh"), beside


def sum_near(rows, fn):
    n = rows.shape[0] // 2
    got = swap(fn(rows[n:]).astype(BF16), "c")
    return fn(rows[:n]) + got.astype(F32)


def quarters_first(v, at):
    for axis, name in ((at, "zh"), (at + 1, "c")):
        v = jnp.where(lax.axis_index(name) == 1, jnp.flip(v, axis=axis), v)
    return v


def relative_tokens(token_order):
    quarter = TOKENS // 4
    own = lax.axis_index("zh") * 2 + lax.axis_index("c")
    token_order = ((token_order // quarter) ^ own) * quarter + token_order % quarter
    order = token_order.reshape(4, 2, 4, 2, 2, TOKENS // 128)
    for dim, name in ((0, "x"), (1, "zl"), (2, "y")):
        n = SIZES[name]
        order = jnp.flip(order, axis=dim)
        order = jnp.concatenate([order, order], axis=dim)
        order = lax.dynamic_slice_in_dim(order, n - 1 - lax.axis_index(name), n, axis=dim)
    return quarters_first(order, 3).transpose(3, 4, 0, 2, 1, 5).reshape(TOKENS)


def body(
    teacher_states,
    layer_map,
    token_order,
    student_states,
    teacher_gain,
    student_gain,
    adapter,
    w_gate,
    w_up,
    w_down,
):
    ff = w_gate.shape[1]
    rows, cols = student_states.shape
    raw = student_states.astype(F32)
    student_sq = jnp.sum(raw * raw, axis=1)
    student_sq = student_sq + swap(student_sq, "c")
    student_sq = student_sq + swap(student_sq, "zh")
    srs = lax.rsqrt(student_sq / D + EPS)
    states = quarters_first(student_states.reshape(2, 2, rows // 4, cols), 0).reshape(4, rows // 4, cols)
    xval = states.astype(F32)
    srs = quarters_first(srs.reshape(2, 2, rows // 4), 0).reshape(4, rows // 4)
    student_normed = (xval * srs[..., None] * student_gain.astype(F32)).astype(BF16)

    xpair = jnp.concatenate([xval, swap(states, "zl").astype(F32)], axis=1)
    normed = jnp.concatenate([student_normed, swap(student_normed, "zl")], axis=1)
    chosen = lax.dynamic_index_in_dim(teacher_states, layer_map[0], 0, keepdims=False)
    chosen, normed = fence((chosen, normed))
    near, srs = gather_near(normed, srs)
    near, beyond = fence((near, swap(chosen, "zh")))
    student_hi = gather_far(near[2:])
    w_both = jnp.concatenate([w_gate, w_up], axis=1)
    order = relative_tokens(token_order)
    chosen_f32 = chosen.astype(F32)
    teacher_sq = jnp.sum(chosen_f32 * chosen_f32, axis=1)
    beside = swap(chosen, "c")
    student_hi, near, w_both, order, teacher_sq, beyond, beside = fence(
        (student_hi, near, w_both, order, teacher_sq, beyond, beside)
    )

    def to_ff(v):
        return dot(v, w_both)

    others = far_blocks(near[:2])
    far, (mine, teacher_sq, beyond) = send_far(student_hi, to_ff, (near[:2], teacher_sq, beyond))
    student_lo = far_rows(mine, others)
    every = ("x", "zl", "y", "zh", "c")
    teacher_sq = jnp.broadcast_to(teacher_sq.reshape(1, 4, 128), (128, 4, 128))
    teacher_sq = lax.all_to_all(teacher_sq, every, 0, 0, tiled=True)
    teacher_sq = jnp.sum(teacher_sq.reshape(32, 2, 2, -1), axis=0)
    trs = lax.rsqrt(quarters_first(teacher_sq, 0).reshape(-1) / DT + EPS)
    teacher_all = jnp.concatenate([chosen, beside, beyond, swap(beyond, "c")], axis=0)
    both = sum_near(student_lo, to_ff)
    teacher_normed = (teacher_all.astype(F32) * trs[:, None] * teacher_gain.astype(F32)).astype(BF16)
    ordered = jnp.take(teacher_normed, order, axis=0)
    both, far, ordered = fence((both, far, ordered))
    target = dot(ordered, adapter)
    both = both + far.astype(F32)
    gate, up = both[:, :ff], both[:, ff:]
    sig = jax.nn.sigmoid(gate)
    hidden = (gate * sig * up).astype(BF16)
    half = TOKENS // 2
    beyond = swap(hidden, "zh")
    hidden_lo = jnp.concatenate([hidden, swap(hidden, "c")], axis=0)
    sum_lo = scatter_far((dot(hidden_lo, w_down) - target[:half]).astype(BF16))
    hidden_hi = jnp.concatenate([beyond, swap(beyond, "c")], axis=0)
    sum_hi = scatter_far((dot(hidden_hi, w_down) - target[half:]).astype(BF16))
    diff = xpair + scatter_near(jnp.concatenate([sum_lo, sum_hi], axis=0))
    grad_out = (diff * (2.0 / TOKENS)).astype(BF16)
    near, _ = gather_near(grad_out, srs)
    grad_out_hi = gather_far(near[2:])
    grad_out_hi, near = fence((grad_out_hi, near))

    def to_hidden(v):
        return lax.dot_general(v, w_down, (((1,), (1,)), ((), ())), preferred_element_type=F32)

    others = far_blocks(near[:2])
    far, mine = send_far(grad_out_hi, to_hidden, near[:2])
    grad_out_lo = far_rows(mine, others)
    grad_hidden = sum_near(grad_out_lo, to_hidden)
    grad_hidden = grad_hidden + far.astype(F32)
    gate_pre = grad_hidden * up * sig * (1.0 + gate * (1.0 - sig))
    up_pre = grad_hidden * gate * sig
    pre = jnp.concatenate([gate_pre, up_pre], axis=1).astype(BF16)
    beyond = swap(pre, "zh")
    other, grad_out_lo = fence((swap(pre, "c"), grad_out_lo))
    pre = jnp.concatenate([pre, other], axis=0)
    grad_out = jnp.concatenate([grad_out_lo, grad_out_hi], axis=0)
    hidden = jnp.concatenate([hidden_lo, hidden_hi], axis=0)
    grad_down = tdot(hidden, grad_out)
    grad_adapter = -tdot(ordered, grad_out)
    first = (tdot(student_lo, pre[:, :ff]), tdot(student_lo, pre[:, ff:]), grad_down, grad_adapter)
    beyond, first = fence((beyond, first))
    pre = jnp.concatenate([beyond, swap(beyond, "c")], axis=0)
    return (
        first[0] + tdot(student_hi, pre[:, :ff]),
        first[1] + tdot(student_hi, pre[:, ff:]),
        first[2],
        first[3],
    )


def solution(mesh):
    fine = Mesh(mesh.devices.reshape(4, 2, 4, 2, 2), tuple(SIZES))
    dp, tensor = ("x", "zl", "y"), ("zh", "c")
    in_specs = (
        P(None, tensor, dp),
        P(),
        P(),
        P(dp, tensor),
        P(dp),
        P(tensor),
        P(dp, tensor),
        P(tensor, dp),
        P(tensor, dp),
        P(dp, tensor),
    )
    out_specs = (P(tensor, dp), P(tensor, dp), P(dp, tensor), P(dp, tensor))
    return jax.shard_map(body, mesh=fine, in_specs=in_specs, out_specs=out_specs, check_vma=False)
```
